32 devices in a mesh: plate: 4 (over z), tower: 4 (over y, core), gz: 2 (over x).
Axes of the slice: x: 2, y: 2, z: 4, core: 2. Of those that a mesh axis runs over, the one named last changes fastest.
Arguments:
- positions: float32 [4, 4, 2, 3, 128], P('plate', 'tower', 'gz'), may hold values from 0 to 1
- features: bfloat16 [4, 4, 2, 576, 128], P('plate', 'tower', 'gz'), may hold values from -6 to 6
- species: int32 [4, 4, 2, 128], P('plate', 'tower', 'gz'), may hold values from 0 to 5
- emb_table: bfloat16 [6, 64], replicated, may hold values from -4 to 4
- edges: int32 [4, 4, 2, 2, 512], P('plate', 'tower', 'gz'), may hold values from 0 to 1151, as said below
- edge_count: int32 [4, 4, 2], P('plate', 'tower', 'gz'), may hold values from 1 to 512, as said below
- w_first: bfloat16 [128, 328], replicated, may hold values from -0.3125 to 0.3125
- w_second: bfloat16 [64, 128], replicated, may hold values from -0.5 to 0.5
- w_out: bfloat16 [64], replicated, may hold values from -0.75 to 0.75
Outputs:
- forces: float32 [4, 4, 2, 3, 128], P('plate', 'tower', 'gz')
- edge_energy: float32 [4, 4, 2, 512], P('plate', 'tower', 'gz')
The draws below stay inside these ranges and needn't reach their ends.
Inputs may be any that keep to these rules, and one draw needn't show every extreme that they name: `edges`: row 0 holds plate-set indices below 384; row 1 holds column-set indices below 1152. Slots at or beyond a box's edge_count are padding with arbitrary valid indices. `edge_count`: some box holds exactly 512 live edges in every draw.
All inputs are finite; a program needn't handle non-finite values.
Results may differ from the reference program's by a relative error of at most 0.011.
Values may be sent and summed in bfloat16 or wider, within the bound.
No kernel may reach another device: no remote copies, remote signals or barrier semaphores. Data moves between devices by JAX's collectives and lax.ppermute only.
A program may use at most 64 MiB of HBM per device.

```python
import math
import jax
import jax.numpy as jnp
from jax import lax

A = 128
E = 512
CH = 64
LAT = 128
RB = 8
S = 6
N_PLATE = 4
N_TOWER = 4
N_GZ = 2


def draw_edges(key, part):
    key_left, key_right = jax.random.split(jax.random.fold_in(key, 11))
    shape = (N_PLATE, N_TOWER, N_GZ, 1, E)
    left_index = jax.random.randint(key_left, shape, 0, 3 * A, dtype=jnp.int32)
    right_index = jax.random.randint(key_right, shape, 0, 9 * A, dtype=jnp.int32)
    return jnp.concatenate([left_index, right_index], axis=3)


def draw_edge_count(key, part):
    key_one, key_two, key_pick = jax.random.split(jax.random.fold_in(key, 23), 3)
    shape = (N_PLATE * N_TOWER * N_GZ,)
    factor_one = jax.random.randint(key_one, shape, 1, E + 1, dtype=jnp.int32)
    factor_two = jax.random.randint(key_two, shape, 1, E + 1, dtype=jnp.int32)
    counts = jnp.maximum(factor_one * factor_two // E, 1)
    chosen = jax.random.randint(key_pick, (), 0, N_PLATE * N_TOWER * N_GZ, dtype=jnp.int32)
    counts = jnp.where(jnp.arange(N_PLATE * N_TOWER * N_GZ, dtype=jnp.int32) == chosen, E, counts)
    return counts.reshape(N_PLATE, N_TOWER, N_GZ).astype(jnp.int32)


def with_ends(drawn, rng, least, largest):
    shape = drawn.shape
    place = [jax.random.randint(jax.random.fold_in(rng, axis), (), 0, shape[axis]) for axis in range(len(shape))]
    drawn = drawn.at[tuple(place)].set(least)
    longest = shape.index(max(shape))
    place[longest] = (place[longest] + 1) % shape[longest]
    return drawn.at[tuple(place)].set(largest)


def block_scale(rng, shape, cuts, least, top_value):
    def one(position, shards_of):
        draws = jax.random.uniform(jax.random.fold_in(jax.random.fold_in(rng, 6), position), (shards_of,), jnp.float32, least / len(cuts), top_value / len(cuts))
        return jnp.repeat(jnp.exp(draws), shape[position] // shards_of).reshape((-1,) + (1,) * (len(shape) - position - 1))

    level = one(*cuts[0])
    for cut in cuts[1:]:
        level = level * one(*cut)
    return level


def centred(key, shape, deviation, limit, cuts=(), kind=jnp.bfloat16):
    loudness = block_scale(key, shape, cuts, -0.22, 0.18) if cuts else 1.0
    array = jax.random.normal(key, shape, jnp.float32) * deviation * loudness
    return jnp.minimum(jnp.maximum(array, -limit), limit).astype(kind)


def setup_inputs(seed: int = 0) -> dict:
    key_list = jax.random.split(jax.random.key(seed), 10)
    positions = jnp.clip(1.0 * jax.random.uniform(key_list[0], (N_PLATE, N_TOWER, N_GZ, 3, A), jnp.float32) ** block_scale(key_list[0], (N_PLATE, N_TOWER, N_GZ, 3, A), ((0, 4), (1, 4), (2, 2)), -0.2, 0.2), 0.0, 1.0)
    features = centred(key_list[1], (N_PLATE, N_TOWER, N_GZ, 9 * CH, A), 1.0, 6.0, ((0, 4), (1, 4), (2, 2)))
    species = with_ends(jax.random.randint(key_list[2], (N_PLATE, N_TOWER, N_GZ, A), 0, S), jax.random.fold_in(key_list[2], 1), 0, S - 1).astype(jnp.int32)
    emb_table = centred(key_list[3], (S, CH), 1.0, 4.0)
    edges = draw_edges(jax.random.fold_in(key_list[9], 71), 0)
    edge_count = draw_edge_count(jax.random.fold_in(key_list[9], 71), 0)
    w_first = centred(key_list[6], (LAT, RB + 5 * CH), (RB + 5 * CH) ** -0.5, 0.3125)
    w_second = centred(key_list[7], (CH, LAT), LAT ** -0.5, 0.5)
    w_out = centred(key_list[8], (CH,), CH ** -0.5, 0.75)
    return dict(positions=positions, features=features, species=species, emb_table=emb_table, edges=edges, edge_count=edge_count, w_first=w_first, w_second=w_second, w_out=w_out)


RADIUS = 3.0
SOFTEN = 0.04

def harmonics(unit_vec):
    cx, cy, cz = (unit_vec[0], unit_vec[1], unit_vec[2])
    root3 = math.sqrt(3.0)
    root15 = math.sqrt(15.0)
    root5 = math.sqrt(5.0)
    return jnp.stack([jnp.ones_like(cx), root3 * cx, root3 * cy, root3 * cz, root15 * cx * cy, root15 * cy * cz, 0.5 * root5 * (3.0 * cz * cz - 1.0), root15 * cx * cz, 0.5 * root15 * (cx * cx - cy * cy)])

def pack_block(positions, features, species, emb_table):
    pos_hi = positions.astype(jnp.bfloat16)
    back = lax.optimization_barrier(pos_hi).astype(jnp.float32)
    pos_lo = (positions - back).astype(jnp.bfloat16)
    kinds = jnp.arange(emb_table.shape[0], dtype=jnp.int32)
    onehot = (species[..., None, :] == kinds[:, None]).astype(jnp.float32)
    emb = jnp.einsum('sc,...sa->...ca', emb_table.astype(jnp.float32), onehot).astype(jnp.bfloat16)
    return jnp.concatenate([features, emb, pos_hi, pos_lo], axis=-2)

def make_offsets(atoms):
    shifts = jnp.arange(3, dtype=jnp.float32) - 1.0
    plate_x = jnp.repeat(shifts, atoms)
    zeros_plate = jnp.zeros_like(plate_x)
    plate_off = jnp.stack([plate_x, zeros_plate, zeros_plate])
    column_y = jnp.repeat(jnp.repeat(shifts, 3), atoms)
    column_z = jnp.repeat(jnp.tile(shifts, 3), atoms)
    column_off = jnp.stack([jnp.zeros_like(column_y), column_y, column_z])
    return (plate_off, column_off)

def degree_sums(terms):
    return jnp.concatenate([terms[0], lax.optimization_barrier(jnp.sum(terms[1:4], 0)), lax.optimization_barrier(jnp.sum(terms[4:9], 0))], 0)

def edge_model(coord_i, coord_j, feat_i, feat_j, emb_i, emb_j, w_first, w_second, w_out):
    width = emb_i.shape[0]
    delta = coord_j - coord_i
    dist2 = lax.optimization_barrier(jnp.sum(delta * delta, 0)) + SOFTEN
    dist = jnp.sqrt(dist2)
    harmonic = harmonics(delta / dist)
    orders = jnp.arange(1, RB + 1, dtype=jnp.float32)
    radial = jnp.sin(orders[:, None] * (math.pi / RADIUS) * dist[None, :]) / dist[None, :]
    envelope = jnp.square(jnp.maximum(1.0 - dist2 / (RADIUS * RADIUS), 0.0))
    proj_i = degree_sums(feat_i.astype(jnp.float32).reshape(9, width, -1) * harmonic[:, None, :])
    proj_j = degree_sums(feat_j.astype(jnp.float32).reshape(9, width, -1) * harmonic[:, None, :])
    inputs = jnp.concatenate([radial, emb_i.astype(jnp.float32), emb_j.astype(jnp.float32), proj_i * proj_j], 0).astype(jnp.bfloat16)
    hidden = jax.nn.silu(jnp.dot(w_first, inputs, preferred_element_type=jnp.float32)).astype(jnp.bfloat16)
    second_layer = jax.nn.silu(jnp.dot(w_second, hidden, preferred_element_type=jnp.float32))
    return envelope * lax.optimization_barrier(jnp.sum(w_out.astype(jnp.float32)[:, None] * second_layer, 0))

def split_rows(picked, offsets, width):
    coord = picked[10 * width:10 * width + 3].astype(jnp.float32) + picked[10 * width + 3:10 * width + 6].astype(jnp.float32) + offsets
    return (coord, picked[:9 * width], picked[9 * width:10 * width])

def device_pass(plate_rows, column_rows, edge_list, live_count, w_first, w_second, w_out, live_only):
    width = (plate_rows.shape[0] - 6) // 10
    atoms = plate_rows.shape[1] // 3
    plate_off, column_off = make_offsets(atoms)
    total = edge_list.shape[-1]
    block = min(1024, total)

    def step(index, carry):
        plate_part, column_part, energy = carry
        start = index * block
        left_index = lax.dynamic_slice_in_dim(edge_list[0], start, block)
        right_index = lax.dynamic_slice_in_dim(edge_list[1], start, block)
        slots = start + jnp.arange(block, dtype=jnp.int32)
        live_mask = (slots < live_count).astype(jnp.float32)
        coord_i, feat_i, emb_i = split_rows(jnp.take(plate_rows, left_index, axis=1), jnp.take(plate_off, left_index, axis=1), width)
        coord_j, feat_j, emb_j = split_rows(jnp.take(column_rows, right_index, axis=1), jnp.take(column_off, right_index, axis=1), width)

        def energy_of(left_coord, right_coord):
            return live_mask * edge_model(left_coord, right_coord, feat_i, feat_j, emb_i, emb_j, w_first, w_second, w_out)
        values, pullback = jax.vjp(energy_of, coord_i, coord_j)
        grad_i, grad_j = pullback(jnp.ones_like(values))
        plate_part = plate_part.at[:, left_index].add(grad_i)
        column_part = column_part.at[:, right_index].add(grad_j)
        energy = lax.dynamic_update_slice_in_dim(energy, values, start, 0)
        return (plate_part, column_part, energy)
    start_carry = (jnp.zeros((3, 3 * atoms), jnp.float32), jnp.zeros((3, 9 * atoms), jnp.float32), jnp.zeros((total,), jnp.float32))
    if live_only:
        upper = (live_count + block - 1) // block
    else:
        upper = total // block
    return lax.fori_loop(0, upper, step, start_carry)

def reference(positions, features, species, emb_table, edges, edge_count, w_first, w_second, w_out):
    packed = pack_block(positions, features, species, emb_table)
    atoms = positions.shape[-1]

    def one_box(forces, device):
        plate = device // (N_TOWER * N_GZ)
        tower = device // N_GZ % N_TOWER
        depth = device % N_GZ
        plate_rows = jnp.concatenate([packed[(plate + shift - 1) % N_PLATE, tower, depth] for shift in range(3)], axis=1)
        column_rows = jnp.concatenate([packed[plate, (tower + row - 1) % N_TOWER, (depth + col - 1) % N_GZ] for row in range(3) for col in range(3)], axis=1)
        plate_part, column_part, energy = device_pass(plate_rows, column_rows, edges[plate, tower, depth], edge_count[plate, tower, depth], w_first, w_second, w_out, False)
        for shift in range(3):
            forces = forces.at[(plate + shift - 1) % N_PLATE, tower, depth].add(-plate_part[:, shift * atoms:(shift + 1) * atoms])
        for row in range(3):
            for col in range(3):
                slot = 3 * row + col
                forces = forces.at[plate, (tower + row - 1) % N_TOWER, (depth + col - 1) % N_GZ].add(-column_part[:, slot * atoms:(slot + 1) * atoms])
        return (forces, energy)
    start_forces = jnp.zeros(positions.shape, jnp.float32)
    forces, energies = lax.scan(one_box, start_forces, jnp.arange(N_PLATE * N_TOWER * N_GZ, dtype=jnp.int32))
    return (forces, energies.reshape(N_PLATE, N_TOWER, N_GZ, edges.shape[-1]))
```

```python
import functools
import math

import jax
import jax.numpy as jnp
from jax import lax
from jax.experimental import pallas as pl
from jax.experimental.pallas import tpu as pltpu
from jax.sharding import PartitionSpec as P

RB = 8
RADIUS = 3.0
SOFTEN = 0.04
EXTRA = 16
F32 = jnp.float32
BF16 = jnp.bfloat16


def fetch(x, axis, shift):
    count = lax.axis_size(axis)
    return lax.ppermute(x, axis, [(i, (i - shift) % count) for i in range(count)])


def distinct(axis):
    count = lax.axis_size(axis)
    shifts, which = [0], []
    for shift in (-1, 0, 1):
        same = [k for k, s in enumerate(shifts) if (s - shift) % count == 0]
        if not same:
            shifts.append(shift)
        which.append(same[0] if same else len(shifts) - 1)
    return shifts, which


def pick(index, table):
    out = jnp.full_like(index, table[0])
    for k in range(1, len(table)):
        if table[k] != table[k - 1]:
            out = out + jnp.where(index >= k, table[k] - table[k - 1], 0)
    return out


def count_steps(index, step, last):
    out = jnp.zeros_like(index)
    for k in range(1, last):
        out = out + jnp.where(index >= k * step, 1, 0)
    return out


def sigmoid(v):
    return 1.0 / (1.0 + jnp.exp(-v))


def edge_kernel(plan, *refs):
    n_plate, n_column, plate_which, tower_which, gz_which, n_gz = plan
    block_refs = refs[: n_plate + n_column]
    (edges_ref, count_ref, emb_ref, w1_ref, w2_ref, wo_ref, energy_ref, plate_ref, column_ref) = refs[
        n_plate + n_column :
    ]
    rows, atoms = block_refs[0].shape
    total = edges_ref.shape[1]
    width = (rows - EXTRA) // 9

    left = edges_ref[0:1, :]
    right = edges_ref[1:2, :]
    side_i = count_steps(left, atoms, 3)
    atom_i = left - side_i * atoms
    row_i = pick(side_i, plate_which) * atoms + atom_i
    blk_j = count_steps(right, atoms, 9)
    atom_j = right - blk_j * atoms
    u_j = jnp.where(blk_j >= 3, 1, 0) + jnp.where(blk_j >= 6, 1, 0)
    v_j = blk_j - 3 * u_j
    row_j = (pick(u_j, tower_which) * n_gz + pick(v_j, gz_which)) * atoms + atom_j

    iota_i = lax.broadcasted_iota(jnp.int32, (n_plate * atoms, total), 0)
    hot_i = jnp.where(iota_i == row_i, 1.0, 0.0).astype(BF16)
    iota_j = lax.broadcasted_iota(jnp.int32, (n_column * atoms, total), 0)
    hot_j = jnp.where(iota_j == row_j, 1.0, 0.0).astype(BF16)

    plate_all = jnp.concatenate([block_refs[k][...] for k in range(n_plate)], axis=1)
    column_all = jnp.concatenate([block_refs[n_plate + k][...] for k in range(n_column)], axis=1)
    got_i = jnp.dot(plate_all, hot_i, preferred_element_type=F32)
    got_j = jnp.dot(column_all, hot_j, preferred_element_type=F32)

    base = 9 * width

    def row(got, k):
        return got[base + k : base + k + 1, :]

    d = []
    for axis in range(3):
        ci = row(got_i, axis) + row(got_i, 3 + axis)
        cj = row(got_j, axis) + row(got_j, 3 + axis)
        off = (None, u_j, v_j)[axis]
        if axis == 0:
            ci = ci + (side_i - 1).astype(F32)
        else:
            cj = cj + (off - 1).astype(F32)
        d.append(cj - ci)
    r2 = d[0] * d[0] + d[1] * d[1] + d[2] * d[2] + SOFTEN
    r = jnp.sqrt(r2)
    inv = 1.0 / r
    nx, ny, nz = d[0] * inv, d[1] * inv, d[2] * inv
    root3, root5, root15 = math.sqrt(3.0), math.sqrt(5.0), math.sqrt(15.0)
    harm = [
        None,
        root3 * nx,
        root3 * ny,
        root3 * nz,
        root15 * nx * ny,
        root15 * ny * nz,
        0.5 * root5 * (3.0 * nz * nz - 1.0),
        root15 * nx * nz,
        0.5 * root15 * (nx * nx - ny * ny),
    ]
    freq = (lax.broadcasted_iota(jnp.int32, (RB, 1), 0) + 1).astype(F32) * (math.pi / RADIUS)
    phase = freq * r
    radial = jnp.sin(phase) * inv
    wave = jnp.cos(phase)
    gap = jnp.maximum(1.0 - r2 / (RADIUS * RADIUS), 0.0)
    env = gap * gap

    def feat(got, m):
        return got[m * width : (m + 1) * width, :]

    def degrees(got):
        one = harm[1] * feat(got, 1) + harm[2] * feat(got, 2) + harm[3] * feat(got, 3)
        two = harm[4] * feat(got, 4)
        for m in range(5, 9):
            two = two + harm[m] * feat(got, m)
        return feat(got, 0), one, two

    s_i = degrees(got_i)
    s_j = degrees(got_j)
    q = jnp.concatenate([(a * b).astype(BF16) for a, b in zip(s_i, s_j)], axis=0)

    kinds = emb_ref.shape[0]
    kind_iota = lax.broadcasted_iota(jnp.int32, (kinds, total), 0).astype(F32)
    tn = (((0,), (0,)), ((), ()))

    def emb_of(got):
        hot = jnp.where(kind_iota == row(got, 6), 1.0, 0.0).astype(BF16)
        return lax.dot_general(emb_ref[...], hot, tn, preferred_element_type=F32).astype(BF16)

    emb = jnp.concatenate([emb_of(got_i), emb_of(got_j)], axis=0)
    w1 = w1_ref[...]
    w_rad = w1[:, :RB]
    w_emb = w1[:, RB : RB + 2 * width]
    w_q = w1[:, RB + 2 * width :]
    pre1 = (
        jnp.dot(w_q, q, preferred_element_type=F32)
        + jnp.dot(w_emb, emb, preferred_element_type=F32)
        + jnp.dot(w_rad, radial.astype(BF16), preferred_element_type=F32)
    )
    sig1 = sigmoid(pre1)
    hidden = (pre1 * sig1).astype(BF16)
    w2 = w2_ref[...]
    pre2 = jnp.dot(w2, hidden, preferred_element_type=F32)
    sig2 = sigmoid(pre2)
    chan = wo_ref.shape[1]
    eye = lax.broadcasted_iota(jnp.int32, (chan, chan), 0) == lax.broadcasted_iota(jnp.int32, (chan, chan), 1)
    w_out = jnp.sum(jnp.where(eye, wo_ref[...].astype(F32), 0.0), axis=1, keepdims=True)
    score = jnp.sum(w_out * (pre2 * sig2), axis=0, keepdims=True)
    slots = lax.broadcasted_iota(jnp.int32, (1, total), 1)
    live = jnp.where(slots < count_ref[0], 1.0, 0.0)
    live_env = live * env
    energy_ref[...] = live_env * score

    g2 = (live_env * w_out) * (sig2 * (1.0 + pre2 * (1.0 - sig2)))
    dh = lax.dot_general(w2, g2.astype(BF16), tn, preferred_element_type=F32).astype(BF16).astype(F32)
    g1 = (dh * (sig1 * (1.0 + pre1 * (1.0 - sig1)))).astype(BF16)
    dq = lax.dot_general(w_q, g1, tn, preferred_element_type=F32).astype(BF16).astype(F32)
    dradial = lax.dot_general(w_rad, g1, tn, preferred_element_type=F32).astype(BF16).astype(F32)
    dy = [None] * 9
    for deg, members in ((1, range(1, 4)), (2, range(4, 9))):
        part = dq[deg * width : (deg + 1) * width, :]
        for_i = part * s_j[deg]
        for_j = part * s_i[deg]
        for m in members:
            dy[m] = jnp.sum(for_i * feat(got_i, m) + for_j * feat(got_j, m), axis=0, keepdims=True)
    gn = [
        root3 * dy[1] + root15 * (ny * dy[4] + nz * dy[7] + nx * dy[8]),
        root3 * dy[2] + root15 * (nx * dy[4] + nz * dy[5] - ny * dy[8]),
        root3 * dy[3] + root15 * (ny * dy[5] + nx * dy[7]) + (3.0 * root5) * nz * dy[6],
    ]
    dr = jnp.sum(dradial * (freq * wave - radial), axis=0, keepdims=True)
    dr = (dr - (gn[0] * nx + gn[1] * ny + gn[2] * nz)) * inv
    dr2 = dr * (0.5 * inv) - (live * score) * gap * (2.0 / (RADIUS * RADIUS))
    grad = jnp.concatenate([gn[k] * inv + 2.0 * d[k] * dr2 for k in range(3)], axis=0)
    high = grad.astype(BF16)
    low = (grad - high.astype(F32)).astype(BF16)
    nt = (((1,), (1,)), ((), ()))

    def spread(hot):
        return lax.dot_general(high, hot, nt, preferred_element_type=F32) + lax.dot_general(
            low, hot, nt, preferred_element_type=F32
        )

    to_plate = spread(hot_i)
    to_column = spread(hot_j)
    own = to_plate[:, :atoms] - to_column[:, :atoms]
    for k in range(1, n_plate):
        plate_ref[k - 1] = to_plate[:, k * atoms : (k + 1) * atoms]
    column_ref[0, 0] = own
    for k in range(1, n_column):
        column_ref[k // n_gz, k % n_gz] = -to_column[:, k * atoms : (k + 1) * atoms]


def shards(positions, features, species, emb_table, edges, edge_count, w_first, w_second, w_out):
    atoms = positions.shape[-1]
    total = edges.shape[-1]
    pos = positions[0, 0, 0]
    high = lax.reduce_precision(pos, 8, 7)
    small = jnp.concatenate(
        [high, pos - high, species[0, 0, 0][None, :].astype(F32), jnp.zeros((EXTRA - 7, atoms), F32)], axis=0
    ).astype(BF16)
    packed = jnp.concatenate([features[0, 0, 0], small], axis=0)

    plate_shifts, plate_which = distinct("plate")
    tower_shifts, tower_which = distinct("tower")
    gz_shifts, gz_which = distinct("gz")
    n_gz = len(gz_shifts)
    plate_blocks = [packed] + [fetch(packed, "plate", s) for s in plate_shifts[1:]]
    gz_blocks = [packed] + [fetch(packed, "gz", s) for s in gz_shifts[1:]]
    column_blocks = list(gz_blocks)
    for s in tower_shifts[1:]:
        column_blocks += [fetch(block, "tower", s) for block in gz_blocks]
    n_plate, n_column = len(plate_blocks), len(column_blocks)

    plan = (n_plate, n_column, plate_which, tower_which, gz_which, n_gz)
    vmem = pl.BlockSpec(memory_space=pltpu.VMEM)
    n_vmem = n_plate + n_column
    energy, plate_part, column_part = pl.pallas_call(
        functools.partial(edge_kernel, plan),
        out_shape=(
            jax.ShapeDtypeStruct((1, total), F32),
            jax.ShapeDtypeStruct((max(n_plate - 1, 1), 3, atoms), F32),
            jax.ShapeDtypeStruct((len(tower_shifts), n_gz, 3, atoms), F32),
        ),
        in_specs=[vmem] * (n_vmem + 1) + [pl.BlockSpec(memory_space=pltpu.SMEM)] + [vmem] * 4,
        out_specs=(vmem, vmem, vmem),
        compiler_params=pltpu.CompilerParams(vmem_limit_bytes=48 * 1024 * 1024),
        name="edge_work",
    )(
        *plate_blocks,
        *column_blocks,
        edges[0, 0, 0],
        edge_count.reshape(1),
        emb_table,
        w_first,
        w_second,
        w_out.reshape(1, -1),
    )

    forces = 0.0
    for k, s in enumerate(plate_shifts[1:]):
        forces = forces + fetch(plate_part[k], "plate", -s)
    column = column_part[:, 0]
    for k, s in enumerate(gz_shifts[1:]):
        column = column + fetch(column_part[:, 1 + k], "gz", -s)
    forces = forces + column[0]
    for k, s in enumerate(tower_shifts[1:]):
        forces = forces + fetch(column[1 + k], "tower", -s)
    return (forces.reshape(1, 1, 1, 3, atoms), energy.reshape(1, 1, 1, -1))


def solution(mesh):
    placed = (
        P("plate", "tower", "gz", None, None),
        P("plate", "tower", "gz", None, None),
        P("plate", "tower", "gz", None),
        P(),
        P("plate", "tower", "gz", None, None),
        P("plate", "tower", "gz"),
        P(),
        P(),
        P(),
    )
    return jax.shard_map(
        shards,
        mesh=mesh,
        in_specs=placed,
        out_specs=(P("plate", "tower", "gz", None, None), P("plate", "tower", "gz", None)),
        check_vma=False,
    )
```

```python
import functools
import math

import jax
import jax.numpy as jnp
from jax import lax
from jax.experimental import pallas as pl
from jax.experimental.pallas import tpu as pltpu
from jax.sharding import PartitionSpec as P

RB = 8
RADIUS = 3.0
SOFTEN = 0.04
EXTRA = 16
F32 = jnp.float32
BF16 = jnp.bfloat16


def moves(axis):
    count = lax.axis_size(axis)
    if count == 1:
        return []
    if count % 2:
        up = [(i, (i + 1) % count) for i in range(count)]
        down = [(i, (i - 1) % count) for i in range(count)]
        return [(up, down), (down, up)]
    first = [(i, i ^ 1) for i in range(count)]
    if count == 2:
        return [(first, first)]
    second = [(i, ((i + 1) if i % 2 else (i - 1)) % count) for i in range(count)]
    return [(first, first), (second, second)]


def which_block(shift, axis, count):
    if count == 1:
        return jnp.zeros_like(shift)
    if count == 2:
        return jnp.where(shift == 1, 0, 1)
    odd = 1 if count % 2 else lax.axis_index(axis) % 2
    return jnp.where(shift == 1, 0, jnp.where(shift == 2, 1 + odd, 2 - odd))


def count_steps(index, step, last):
    out = jnp.zeros_like(index)
    for k in range(1, last):
        out = out + jnp.where(index >= k * step, 1, 0)
    return out


def sigmoid(v):
    return 1.0 / (1.0 + jnp.exp(-v))


def pack_kernel(pos_ref, feat_ref, kind_ref, out_ref, pos_vmem, kind_vmem, sems):
    rows, atoms = feat_ref.shape
    copies = [
        pltpu.make_async_copy(pos_ref, pos_vmem, sems.at[0]),
        pltpu.make_async_copy(kind_ref, kind_vmem, sems.at[1]),
        pltpu.make_async_copy(feat_ref, out_ref.at[pl.ds(0, rows)], sems.at[2]),
    ]
    for copy in copies:
        copy.start()
    copies[0].wait()
    copies[1].wait()
    pos = jnp.concatenate([pos_vmem[k] for k in range(3)], axis=0)
    high = pos.astype(BF16).astype(F32)
    fill = jnp.zeros((EXTRA - 7, atoms), F32)
    small = jnp.concatenate([high, pos - high, kind_vmem[...].astype(F32), fill], axis=0)
    out_ref[pl.ds(rows, EXTRA), :] = small.astype(BF16)
    copies[2].wait()


def pack(positions, features, species):
    rows, atoms = features.shape
    hbm = pl.BlockSpec(memory_space=pltpu.HBM)
    return pl.pallas_call(
        pack_kernel,
        out_shape=jax.ShapeDtypeStruct((rows + EXTRA, atoms), BF16),
        in_specs=[hbm, hbm, hbm],
        out_specs=pl.BlockSpec(memory_space=pltpu.VMEM),
        scratch_shapes=[
            pltpu.VMEM(positions.shape, F32),
            pltpu.VMEM(species.shape, jnp.int32),
            pltpu.SemaphoreType.DMA((3,)),
        ],
        compiler_params=pltpu.CompilerParams(vmem_limit_bytes=4 * 1024 * 1024),
        name="pack",
    )(positions, features, species)


def prep_kernel(plan, edges_hbm, count_ref, emb_hbm, w1_hbm, w2_hbm, wo_hbm, after_ref, *refs):
    n_plate, n_column, n_gz, counts, atoms = plan
    hot_i_ref, hot_j_ref, side_ref, emb_ref, w1_ref, w2_ref, wo_ref, edges_ref, row_ref, sems = refs
    pairs = ((edges_hbm, edges_ref), (emb_hbm, emb_ref), (w1_hbm, w1_ref), (w2_hbm, w2_ref), (wo_hbm, row_ref))
    copies = [pltpu.make_async_copy(src, dst, sems.at[k]) for k, (src, dst) in enumerate(pairs)]
    for copy in copies:
        copy.start()
    for copy in copies:
        copy.wait()
    total = edges_ref.shape[1]
    left = edges_ref[0:1, :]
    right = edges_ref[1:2, :]
    side_i = count_steps(left, atoms, 3)
    row_i = which_block(side_i, "plate", counts[0]) * atoms + (left - side_i * atoms)
    blk_j = count_steps(right, atoms, 9)
    u_j = count_steps(blk_j, 3, 3)
    v_j = blk_j - 3 * u_j
    slot_j = which_block(u_j, "tower", counts[1]) * n_gz + which_block(v_j, "gz", counts[2])
    row_j = slot_j * atoms + (right - blk_j * atoms)
    iota_i = lax.broadcasted_iota(jnp.int32, (n_plate * atoms, total), 0)
    hot_i_ref[...] = jnp.where(iota_i == row_i, 1.0, 0.0).astype(BF16)
    iota_j = lax.broadcasted_iota(jnp.int32, (n_column * atoms, total), 0)
    hot_j_ref[...] = jnp.where(iota_j == row_j, 1.0, 0.0).astype(BF16)
    slots = lax.broadcasted_iota(jnp.int32, (1, total), 1)
    live = jnp.where(slots < count_ref[0], 1, 0)
    side_ref[...] = jnp.concatenate([side_i - 1, u_j - 1, v_j - 1, live] * 2, axis=0).astype(F32)
    chan = row_ref.shape[1]
    eye = lax.broadcasted_iota(jnp.int32, (chan, chan), 0) == lax.broadcasted_iota(jnp.int32, (chan, chan), 1)
    wo_ref[...] = jnp.sum(jnp.where(eye, row_ref[...].astype(F32), 0.0), axis=1, keepdims=True)


def edge_kernel(plan, *refs):
    n_plate, n_column, n_gz, counts, atoms = plan
    block_refs = refs[: n_plate + n_column]
    (hot_i_ref, hot_j_ref, side_ref, emb_ref, w1_ref, w2_ref, wo_ref) = refs[n_plate + n_column : n_plate + n_column + 7]
    energy_ref, plate_ref, column_ref = refs[n_plate + n_column + 7 :]
    rows = block_refs[0].shape[0]
    total = hot_i_ref.shape[1]
    width = (rows - EXTRA) // 9
    hot_i = hot_i_ref[...]
    hot_j = hot_j_ref[...]

    plate_all = jnp.concatenate([block_refs[k][...] for k in range(n_plate)], axis=1)
    column_all = jnp.concatenate([block_refs[n_plate + k][...] for k in range(n_column)], axis=1)
    got_i = jnp.dot(plate_all, hot_i, preferred_element_type=F32)
    got_j = jnp.dot(column_all, hot_j, preferred_element_type=F32)

    base = 9 * width

    def row(got, k):
        return got[base + k : base + k + 1, :]

    d = []
    for axis in range(3):
        ci = row(got_i, axis) + row(got_i, 3 + axis)
        cj = row(got_j, axis) + row(got_j, 3 + axis)
        off = side_ref[axis : axis + 1, :]
        if axis == 0:
            ci = ci + off
        else:
            cj = cj + off
        d.append(cj - ci)
    r2 = d[0] * d[0] + d[1] * d[1] + d[2] * d[2] + SOFTEN
    r = jnp.sqrt(r2)
    inv = 1.0 / r
    nx, ny, nz = d[0] * inv, d[1] * inv, d[2] * inv
    root3, root5, root15 = math.sqrt(3.0), math.sqrt(5.0), math.sqrt(15.0)
    harm = [
        None,
        root3 * nx,
        root3 * ny,
        root3 * nz,
        root15 * nx * ny,
        root15 * ny * nz,
        0.5 * root5 * (3.0 * nz * nz - 1.0),
        root15 * nx * nz,
        0.5 * root15 * (nx * nx - ny * ny),
    ]
    freq = (lax.broadcasted_iota(jnp.int32, (RB, 1), 0) + 1).astype(F32) * (math.pi / RADIUS)
    phase = freq * r
    radial = jnp.sin(phase) * inv
    wave = jnp.cos(phase)
    gap = jnp.maximum(1.0 - r2 / (RADIUS * RADIUS), 0.0)
    env = gap * gap

    def feat(got, m):
        return got[m * width : (m + 1) * width, :]

    def degrees(got):
        one = harm[1] * feat(got, 1) + harm[2] * feat(got, 2) + harm[3] * feat(got, 3)
        two = harm[4] * feat(got, 4)
        for m in range(5, 9):
            two = two + harm[m] * feat(got, m)
        return feat(got, 0), one, two

    s_i = degrees(got_i)
    s_j = degrees(got_j)
    q = jnp.concatenate([(a * b).astype(BF16) for a, b in zip(s_i, s_j)], axis=0)

    kinds = emb_ref.shape[0]
    kind_iota = lax.broadcasted_iota(jnp.int32, (kinds, total), 0).astype(F32)
    tn = (((0,), (0,)), ((), ()))

    def emb_of(got):
        hot = jnp.where(kind_iota == row(got, 6), 1.0, 0.0).astype(BF16)
        return lax.dot_general(emb_ref[...], hot, tn, preferred_element_type=F32).astype(BF16)

    emb = jnp.concatenate([emb_of(got_i), emb_of(got_j)], axis=0)
    w1 = w1_ref[...]
    w_rad = w1[:RB, :]
    w_emb = w1[RB : RB + 2 * width, :]
    w_q = w1[RB + 2 * width :, :]
    pre1 = (
        lax.dot_general(w_q, q, tn, preferred_element_type=F32)
        + lax.dot_general(w_emb, emb, tn, preferred_element_type=F32)
        + lax.dot_general(w_rad, radial.astype(BF16), tn, preferred_element_type=F32)
    )
    sig1 = sigmoid(pre1)
    hidden = (pre1 * sig1).astype(BF16)
    w2 = w2_ref[...]
    pre2 = jnp.dot(w2, hidden, preferred_element_type=F32)
    sig2 = sigmoid(pre2)
    w_out = wo_ref[...]
    score = jnp.sum(w_out * (pre2 * sig2), axis=0, keepdims=True)
    live = side_ref[3:4, :]
    live_env = live * env
    energy_ref[...] = live_env * score

    g2 = (live_env * w_out) * (sig2 * (1.0 + pre2 * (1.0 - sig2)))
    dh = lax.dot_general(w2, g2.astype(BF16), tn, preferred_element_type=F32).astype(BF16).astype(F32)
    g1 = (dh * (sig1 * (1.0 + pre1 * (1.0 - sig1)))).astype(BF16)
    dq = jnp.dot(w_q, g1, preferred_element_type=F32).astype(BF16).astype(F32)
    dradial = jnp.dot(w_rad, g1, preferred_element_type=F32).astype(BF16).astype(F32)
    dy = [None] * 9
    for deg, members in ((1, range(1, 4)), (2, range(4, 9))):
        part = dq[deg * width : (deg + 1) * width, :]
        for_i = part * s_j[deg]
        for_j = part * s_i[deg]
        for m in members:
            dy[m] = jnp.sum(for_i * feat(got_i, m) + for_j * feat(got_j, m), axis=0, keepdims=True)
    gn = [
        root3 * dy[1] + root15 * (ny * dy[4] + nz * dy[7] + nx * dy[8]),
        root3 * dy[2] + root15 * (nx * dy[4] + nz * dy[5] - ny * dy[8]),
        root3 * dy[3] + root15 * (ny * dy[5] + nx * dy[7]) + (3.0 * root5) * nz * dy[6],
    ]
    dr = jnp.sum(dradial * (freq * wave - radial), axis=0, keepdims=True)
    dr = (dr - (gn[0] * nx + gn[1] * ny + gn[2] * nz)) * inv
    dr2 = dr * (0.5 * inv) - (live * score) * gap * (2.0 / (RADIUS * RADIUS))
    grad = jnp.concatenate([gn[k] * inv + 2.0 * d[k] * dr2 for k in range(3)], axis=0)
    high = grad.astype(BF16).astype(F32)
    both = jnp.concatenate([high, grad - high, jnp.zeros((10, total), F32)], axis=0).astype(BF16)
    nt = (((1,), (1,)), ((), ()))

    def spread(hot):
        out = lax.dot_general(both, hot, nt, preferred_element_type=F32)
        return out[0:3, :] + out[3:6, :]

    to_plate = spread(hot_i)
    to_column = spread(hot_j)
    own = to_plate[:, :atoms] - to_column[:, :atoms]
    for k in range(1, n_plate):
        plate_ref[k - 1] = to_plate[:, k * atoms : (k + 1) * atoms]
    column_ref[0, 0] = own
    for k in range(1, n_column):
        column_ref[k // n_gz, k % n_gz] = -to_column[:, k * atoms : (k + 1) * atoms]


def shards(positions, features, species, emb_table, edges, edge_count, w_first, w_second, w_out):
    atoms = positions.shape[-1]
    total = edges.shape[-1]
    packed = pack(positions.reshape(3, 1, atoms), features[0, 0, 0], species[0, 0])

    plate_moves, tower_moves, gz_moves = moves("plate"), moves("tower"), moves("gz")
    n_gz = 1 + len(gz_moves)
    plate_blocks = [packed] + [lax.ppermute(packed, "plate", there) for there, _ in plate_moves]
    gz_blocks = [packed] + [lax.ppermute(packed, "gz", there) for there, _ in gz_moves]
    far = [[lax.ppermute(b, "tower", there) for b in gz_blocks] for there, _ in tower_moves[1:]]
    near = [[lax.ppermute(b, "tower", there) for b in gz_blocks] for there, _ in tower_moves[:1]]
    column_blocks = gz_blocks + [b for blocks in near + far for b in blocks]
    n_plate, n_column = len(plate_blocks), len(column_blocks)

    counts = (lax.axis_size("plate"), lax.axis_size("tower"), lax.axis_size("gz"))
    plan = (n_plate, n_column, n_gz, counts, atoms)
    vmem = pl.BlockSpec(memory_space=pltpu.VMEM)
    hbm = pl.BlockSpec(memory_space=pltpu.HBM)
    smem = pl.BlockSpec(memory_space=pltpu.SMEM)
    w_table = w_first.T
    w_row = w_out.reshape(1, -1)
    edge_list = edges[0, 0, 0]
    prepared = pl.pallas_call(
        functools.partial(prep_kernel, plan),
        out_shape=(
            jax.ShapeDtypeStruct((n_plate * atoms, total), BF16),
            jax.ShapeDtypeStruct((n_column * atoms, total), BF16),
            jax.ShapeDtypeStruct((8, total), F32),
            jax.ShapeDtypeStruct(emb_table.shape, BF16),
            jax.ShapeDtypeStruct(w_table.shape, BF16),
            jax.ShapeDtypeStruct(w_second.shape, BF16),
            jax.ShapeDtypeStruct((w_row.shape[1], 1), F32),
        ),
        in_specs=[hbm, smem, hbm, hbm, hbm, hbm, pl.BlockSpec(memory_space=pl.ANY)],
        out_specs=(vmem,) * 7,
        scratch_shapes=[
            pltpu.VMEM(edge_list.shape, jnp.int32),
            pltpu.VMEM(w_row.shape, BF16),
            pltpu.SemaphoreType.DMA((5,)),
        ],
        compiler_params=pltpu.CompilerParams(vmem_limit_bytes=8 * 1024 * 1024),
        name="prep",
    )(edge_list, edge_count.reshape(1), emb_table, w_table, w_second, w_row, gz_blocks[-1])
    energy, plate_part, column_part = pl.pallas_call(
        functools.partial(edge_kernel, plan),
        out_shape=(
            jax.ShapeDtypeStruct((1, total), F32),
            jax.ShapeDtypeStruct((max(n_plate - 1, 1), 3, atoms), F32),
            jax.ShapeDtypeStruct((1 + len(tower_moves), n_gz, 3, atoms), F32),
        ),
        in_specs=[vmem] * (n_plate + n_column + 7),
        out_specs=(vmem, vmem, vmem),
        compiler_params=pltpu.CompilerParams(vmem_limit_bytes=32 * 1024 * 1024),
        name="edge_work",
    )(*plate_blocks, *column_blocks, *prepared)

    forces = 0.0
    for k, (_, back) in enumerate(plate_moves):
        forces = forces + lax.ppermute(plate_part[k], "plate", back)
    column = column_part[:, 0]
    for k, (_, back) in enumerate(gz_moves):
        column = column + lax.ppermute(column_part[:, 1 + k], "gz", back)
    forces = forces + column[0]
    for k, (_, back) in enumerate(tower_moves):
        forces = forces + lax.ppermute(column[1 + k], "tower", back)
    return (forces.reshape(1, 1, 1, 3, atoms), energy.reshape(1, 1, 1, -1))


def solution(mesh):
    placed = (
        P("plate", "tower", "gz", None, None),
        P("plate", "tower", "gz", None, None),
        P("plate", "tower", "gz", None),
        P(),
        P("plate", "tower", "gz", None, None),
        P("plate", "tower", "gz"),
        P(),
        P(),
        P(),
    )
    return jax.shard_map(
        shards,
        mesh=mesh,
        in_specs=placed,
        out_specs=(P("plate", "tower", "gz", None, None), P("plate", "tower", "gz", None)),
        check_vma=False,
    )
```

```python
import functools
import math

import jax
import jax.numpy as jnp
from jax import lax
from jax.experimental import pallas as pl
from jax.experimental.pallas import tpu as pltpu
from jax.sharding import PartitionSpec as P

RB = 8
RADIUS = 3.0
SOFTEN = 0.04
EXTRA = 16
F32 = jnp.float32
BF16 = jnp.bfloat16


def moves(axis):
    count = lax.axis_size(axis)
    if count == 1:
        return []
    if count % 2:
        up = [(i, (i + 1) % count) for i in range(count)]
        down = [(i, (i - 1) % count) for i in range(count)]
        return [(up, down), (down, up)]
    first = [(i, i ^ 1) for i in range(count)]
    if count == 2:
        return [(first, first)]
    second = [(i, ((i + 1) if i % 2 else (i - 1)) % count) for i in range(count)]
    return [(first, first), (second, second)]


def which_block(shift, axis, count):
    if count == 1:
        return jnp.zeros_like(shift)
    if count == 2:
        return jnp.where(shift == 1, 0, 1)
    odd = 1 if count % 2 else lax.axis_index(axis) % 2
    return jnp.where(shift == 1, 0, jnp.where(shift == 2, 1 + odd, 2 - odd))


def count_steps(index, step, last):
    out = jnp.zeros_like(index)
    for k in range(1, last):
        out = out + jnp.where(index >= k * step, 1, 0)
    return out


def sigmoid(v):
    return 1.0 / (1.0 + jnp.exp(-v))


def pack_kernel(pos_ref, feat_ref, kind_ref, out_ref, pos_vmem, kind_vmem, sems):
    rows, atoms = feat_ref.shape
    copies = [
        pltpu.make_async_copy(pos_ref, pos_vmem, sems.at[0]),
        pltpu.make_async_copy(kind_ref, kind_vmem, sems.at[1]),
        pltpu.make_async_copy(feat_ref, out_ref.at[pl.ds(0, rows)], sems.at[2]),
    ]
    for copy in copies:
        copy.start()
    copies[0].wait()
    copies[1].wait()
    pos = jnp.concatenate([pos_vmem[k] for k in range(3)], axis=0)
    high = pos.astype(BF16).astype(F32)
    fill = jnp.zeros((EXTRA - 7, atoms), F32)
    small = jnp.concatenate([high, pos - high, kind_vmem[...].astype(F32), fill], axis=0)
    out_ref[pl.ds(rows, EXTRA), :] = small.astype(BF16)
    copies[2].wait()


def pack(positions, features, species):
    rows, atoms = features.shape
    hbm = pl.BlockSpec(memory_space=pltpu.HBM)
    return pl.pallas_call(
        pack_kernel,
        out_shape=jax.ShapeDtypeStruct((rows + EXTRA, atoms), BF16),
        in_specs=[hbm, hbm, hbm],
        out_specs=pl.BlockSpec(memory_space=pltpu.VMEM),
        scratch_shapes=[
            pltpu.VMEM(positions.shape, F32),
            pltpu.VMEM(species.shape, jnp.int32),
            pltpu.SemaphoreType.DMA((3,)),
        ],
        compiler_params=pltpu.CompilerParams(vmem_limit_bytes=4 * 1024 * 1024),
        name="pack",
    )(*(pltpu.with_memory_space_constraint(x, pltpu.HBM) for x in (positions, features, species)))


def prep_kernel(plan, edges_hbm, count_ref, emb_hbm, w1_hbm, w2_hbm, wo_hbm, after_ref, *refs):
    n_plate, n_column, n_gz, counts, atoms = plan
    hot_i_ref, hot_j_ref, side_ref, emb_ref, w1_ref, w2_ref, wo_ref, edges_ref, row_ref, sems = refs
    pairs = ((edges_hbm, edges_ref), (emb_hbm, emb_ref), (w1_hbm, w1_ref), (w2_hbm, w2_ref), (wo_hbm, row_ref))
    copies = [pltpu.make_async_copy(src, dst, sems.at[k]) for k, (src, dst) in enumerate(pairs)]
    for copy in copies:
        copy.start()
    for copy in copies:
        copy.wait()
    total = edges_ref.shape[1]
    left = edges_ref[0:1, :]
    right = edges_ref[1:2, :]
    side_i = count_steps(left, atoms, 3)
    row_i = which_block(side_i, "plate", counts[0]) * atoms + (left - side_i * atoms)
    blk_j = count_steps(right, atoms, 9)
    u_j = count_steps(blk_j, 3, 3)
    v_j = blk_j - 3 * u_j
    slot_j = which_block(u_j, "tower", counts[1]) * n_gz + which_block(v_j, "gz", counts[2])
    row_j = slot_j * atoms + (right - blk_j * atoms)
    iota_i = lax.broadcasted_iota(jnp.int32, (n_plate * atoms, total), 0)
    hot_i_ref[...] = jnp.where(iota_i == row_i, 1.0, 0.0).astype(BF16)
    iota_j = lax.broadcasted_iota(jnp.int32, (n_column * atoms, total), 0)
    hot_j_ref[...] = jnp.where(iota_j == row_j, 1.0, 0.0).astype(BF16)
    slots = lax.broadcasted_iota(jnp.int32, (1, total), 1)
    live = jnp.where(slots < count_ref[0], 1, 0)
    side_ref[...] = jnp.concatenate([side_i - 1, u_j - 1, v_j - 1, live] * 2, axis=0).astype(F32)
    chan = row_ref.shape[1]
    eye = lax.broadcasted_iota(jnp.int32, (chan, chan), 0) == lax.broadcasted_iota(jnp.int32, (chan, chan), 1)
    wo_ref[...] = jnp.sum(jnp.where(eye, row_ref[...].astype(F32), 0.0), axis=1, keepdims=True)


def edge_kernel(plan, *refs):
    n_plate, n_column, n_gz, counts, atoms = plan
    n_far = n_column - n_gz
    block_refs = refs[n_column : n_plate + n_column] + refs[n_far:n_column] + refs[:n_far]
    (hot_i_ref, hot_j_ref, side_ref, emb_ref, w1_ref, w2_ref, wo_ref) = refs[n_plate + n_column : n_plate + n_column + 7]
    energy_ref, plate_ref, column_ref = refs[n_plate + n_column + 7 :]
    rows = block_refs[0].shape[0]
    total = hot_i_ref.shape[1]
    width = (rows - EXTRA) // 9
    hot_i = hot_i_ref[...]
    hot_j = hot_j_ref[...]

    plate_all = jnp.concatenate([block_refs[k][...] for k in range(n_plate)], axis=1)
    column_all = jnp.concatenate([block_refs[n_plate + k][...] for k in range(n_column)], axis=1)
    got_i = jnp.dot(plate_all, hot_i, preferred_element_type=F32)
    got_j = jnp.dot(column_all, hot_j, preferred_element_type=F32)

    base = 9 * width

    def row(got, k):
        return got[base + k : base + k + 1, :]

    d = []
    for axis in range(3):
        ci = row(got_i, axis) + row(got_i, 3 + axis)
        cj = row(got_j, axis) + row(got_j, 3 + axis)
        off = side_ref[axis : axis + 1, :]
        if axis == 0:
            ci = ci + off
        else:
            cj = cj + off
        d.append(cj - ci)
    r2 = d[0] * d[0] + d[1] * d[1] + d[2] * d[2] + SOFTEN
    r = jnp.sqrt(r2)
    inv = 1.0 / r
    nx, ny, nz = d[0] * inv, d[1] * inv, d[2] * inv
    root3, root5, root15 = math.sqrt(3.0), math.sqrt(5.0), math.sqrt(15.0)
    harm = [
        None,
        root3 * nx,
        root3 * ny,
        root3 * nz,
        root15 * nx * ny,
        root15 * ny * nz,
        0.5 * root5 * (3.0 * nz * nz - 1.0),
        root15 * nx * nz,
        0.5 * root15 * (nx * nx - ny * ny),
    ]
    freq = (lax.broadcasted_iota(jnp.int32, (RB, 1), 0) + 1).astype(F32) * (math.pi / RADIUS)
    phase = freq * r
    radial = jnp.sin(phase) * inv
    wave = jnp.cos(phase)
    gap = jnp.maximum(1.0 - r2 / (RADIUS * RADIUS), 0.0)
    env = gap * gap

    def feat(got, m):
        return got[m * width : (m + 1) * width, :]

    def degrees(got):
        one = harm[1] * feat(got, 1) + harm[2] * feat(got, 2) + harm[3] * feat(got, 3)
        two = harm[4] * feat(got, 4)
        for m in range(5, 9):
            two = two + harm[m] * feat(got, m)
        return feat(got, 0), one, two

    s_i = degrees(got_i)
    s_j = degrees(got_j)
    q = jnp.concatenate([(a * b).astype(BF16) for a, b in zip(s_i, s_j)], axis=0)

    kinds = emb_ref.shape[0]
    kind_iota = lax.broadcasted_iota(jnp.int32, (kinds, total), 0).astype(F32)
    tn = (((0,), (0,)), ((), ()))

    def emb_of(got):
        hot = jnp.where(kind_iota == row(got, 6), 1.0, 0.0).astype(BF16)
        return lax.dot_general(emb_ref[...], hot, tn, preferred_element_type=F32).astype(BF16)

    emb = jnp.concatenate([emb_of(got_i), emb_of(got_j)], axis=0)
    w1 = w1_ref[...]
    w_rad = w1[:RB, :]
    w_emb = w1[RB : RB + 2 * width, :]
    w_q = w1[RB + 2 * width :, :]
    pre1 = (
        lax.dot_general(w_q, q, tn, preferred_element_type=F32)
        + lax.dot_general(w_emb, emb, tn, preferred_element_type=F32)
        + lax.dot_general(w_rad, radial.astype(BF16), tn, preferred_element_type=F32)
    )
    sig1 = sigmoid(pre1)
    hidden = (pre1 * sig1).astype(BF16)
    w2 = w2_ref[...]
    pre2 = jnp.dot(w2, hidden, preferred_element_type=F32)
    sig2 = sigmoid(pre2)
    w_out = wo_ref[...]
    score = jnp.sum(w_out * (pre2 * sig2), axis=0, keepdims=True)
    live = side_ref[3:4, :]
    live_env = live * env
    energy_ref[...] = live_env * score

    g2 = (live_env * w_out) * (sig2 * (1.0 + pre2 * (1.0 - sig2)))
    dh = lax.dot_general(w2, g2.astype(BF16), tn, preferred_element_type=F32).astype(BF16).astype(F32)
    g1 = (dh * (sig1 * (1.0 + pre1 * (1.0 - sig1)))).astype(BF16)
    dq = jnp.dot(w_q, g1, preferred_element_type=F32).astype(BF16).astype(F32)
    dradial = jnp.dot(w_rad, g1, preferred_element_type=F32).astype(BF16).astype(F32)
    dy = [None] * 9
    for deg, members in ((1, range(1, 4)), (2, range(4, 9))):
        part = dq[deg * width : (deg + 1) * width, :]
        for_i = part * s_j[deg]
        for_j = part * s_i[deg]
        for m in members:
            dy[m] = jnp.sum(for_i * feat(got_i, m) + for_j * feat(got_j, m), axis=0, keepdims=True)
    gn = [
        root3 * dy[1] + root15 * (ny * dy[4] + nz * dy[7] + nx * dy[8]),
        root3 * dy[2] + root15 * (nx * dy[4] + nz * dy[5] - ny * dy[8]),
        root3 * dy[3] + root15 * (ny * dy[5] + nx * dy[7]) + (3.0 * root5) * nz * dy[6],
    ]
    dr = jnp.sum(dradial * (freq * wave - radial), axis=0, keepdims=True)
    dr = (dr - (gn[0] * nx + gn[1] * ny + gn[2] * nz)) * inv
    dr2 = dr * (0.5 * inv) - (live * score) * gap * (2.0 / (RADIUS * RADIUS))
    grad = jnp.concatenate([gn[k] * inv + 2.0 * d[k] * dr2 for k in range(3)], axis=0)
    high = grad.astype(BF16).astype(F32)
    both = jnp.concatenate([high, grad - high, jnp.zeros((10, total), F32)], axis=0).astype(BF16)
    nt = (((1,), (1,)), ((), ()))

    def spread(hot):
        out = lax.dot_general(both, hot, nt, preferred_element_type=F32)
        return out[0:3, :] + out[3:6, :]

    to_plate = spread(hot_i)
    to_column = spread(hot_j)
    own = to_plate[:, :atoms] - to_column[:, :atoms]
    for k in range(1, n_plate):
        plate_ref[k - 1] = to_plate[:, k * atoms : (k + 1) * atoms]
    column_ref[0, 0] = own
    for k in range(1, n_column):
        column_ref[k // n_gz, k % n_gz] = -to_column[:, k * atoms : (k + 1) * atoms]


def shards(positions, features, species, emb_table, edges, edge_count, w_first, w_second, w_out):
    atoms = positions.shape[-1]
    total = edges.shape[-1]
    packed = pack(positions.reshape(3, 1, atoms), features[0, 0, 0], species[0, 0])

    plate_moves, tower_moves, gz_moves = moves("plate"), moves("tower"), moves("gz")
    n_gz = 1 + len(gz_moves)
    plate_blocks = [packed] + [lax.ppermute(packed, "plate", there) for there, _ in plate_moves]
    gz_blocks = [packed] + [lax.ppermute(packed, "gz", there) for there, _ in gz_moves]
    near = [[lax.ppermute(b, "tower", there) for b in gz_blocks] for there, _ in tower_moves[:1]]
    relay = list(gz_blocks)
    if near and gz_moves:
        relay[1:] = lax.optimization_barrier((*gz_blocks[1:], near[0][0]))[:-1]
    far = [[lax.ppermute(b, "tower", there) for b in relay] for there, _ in tower_moves[1:]]
    column_blocks = gz_blocks + [b for blocks in near + far for b in blocks]
    n_plate, n_column = len(plate_blocks), len(column_blocks)

    counts = (lax.axis_size("plate"), lax.axis_size("tower"), lax.axis_size("gz"))
    plan = (n_plate, n_column, n_gz, counts, atoms)
    vmem = pl.BlockSpec(memory_space=pltpu.VMEM)
    hbm = pl.BlockSpec(memory_space=pltpu.HBM)
    smem = pl.BlockSpec(memory_space=pltpu.SMEM)
    w_table = w_first.T
    w_row = w_out.reshape(1, -1)
    edge_list = edges[0, 0, 0]
    prepared = pl.pallas_call(
        functools.partial(prep_kernel, plan),
        out_shape=(
            jax.ShapeDtypeStruct((n_plate * atoms, total), BF16),
            jax.ShapeDtypeStruct((n_column * atoms, total), BF16),
            jax.ShapeDtypeStruct((8, total), F32),
            jax.ShapeDtypeStruct(emb_table.shape, BF16),
            jax.ShapeDtypeStruct(w_table.shape, BF16),
            jax.ShapeDtypeStruct(w_second.shape, BF16),
            jax.ShapeDtypeStruct((w_row.shape[1], 1), F32),
        ),
        in_specs=[hbm, smem, hbm, hbm, hbm, hbm, pl.BlockSpec(memory_space=pl.ANY)],
        out_specs=(vmem,) * 7,
        scratch_shapes=[
            pltpu.VMEM(edge_list.shape, jnp.int32),
            pltpu.VMEM(w_row.shape, BF16),
            pltpu.SemaphoreType.DMA((5,)),
        ],
        compiler_params=pltpu.CompilerParams(vmem_limit_bytes=8 * 1024 * 1024),
        name="prep",
    )(
        pltpu.with_memory_space_constraint(edge_list, pltpu.HBM),
        edge_count.reshape(1),
        *(pltpu.with_memory_space_constraint(w, pltpu.HBM) for w in (emb_table, w_table, w_second, w_row)),
        gz_blocks[-1],
    )
    energy, plate_part, column_part = pl.pallas_call(
        functools.partial(edge_kernel, plan),
        out_shape=(
            jax.ShapeDtypeStruct((1, total), F32),
            jax.ShapeDtypeStruct((max(n_plate - 1, 1), 3, atoms), F32),
            jax.ShapeDtypeStruct((1 + len(tower_moves), n_gz, 3, atoms), F32),
        ),
        in_specs=[vmem] * (n_plate + n_column + 7),
        out_specs=(vmem, vmem, vmem),
        compiler_params=pltpu.CompilerParams(vmem_limit_bytes=32 * 1024 * 1024),
        name="edge_work",
    )(*column_blocks[n_gz:], *column_blocks[:n_gz], *plate_blocks, *prepared)

    forces = 0.0
    for k, (_, back) in enumerate(plate_moves):
        forces = forces + lax.ppermute(plate_part[k], "plate", back)
    column = column_part[:, 0]
    for k, (_, back) in enumerate(gz_moves):
        column = column + lax.ppermute(column_part[:, 1 + k], "gz", back)
    forces = forces + column[0]
    for k, (_, back) in enumerate(tower_moves):
        forces = forces + lax.ppermute(column[1 + k], "tower", back)
    return (forces.reshape(1, 1, 1, 3, atoms), energy.reshape(1, 1, 1, -1))


def solution(mesh):
    placed = (
        P("plate", "tower", "gz", None, None),
        P("plate", "tower", "gz", None, None),
        P("plate", "tower", "gz", None),
        P(),
        P("plate", "tower", "gz", None, None),
        P("plate", "tower", "gz"),
        P(),
        P(),
        P(),
    )
    return jax.shard_map(
        shards,
        mesh=mesh,
        in_specs=placed,
        out_specs=(P("plate", "tower", "gz", None, None), P("plate", "tower", "gz", None)),
        check_vma=False,
    )
```

```python
import functools
import math

import jax
import jax.numpy as jnp
from jax import lax
from jax.experimental import pallas as pl
from jax.experimental.pallas import tpu as pltpu
from jax.sharding import PartitionSpec as P

RB = 8
RADIUS = 3.0
SOFTEN = 0.04
EXTRA = 16
F32 = jnp.float32
BF16 = jnp.bfloat16


def moves(axis):
    count = lax.axis_size(axis)
    if count == 1:
        return []
    if count % 2:
        up = [(i, (i + 1) % count) for i in range(count)]
        down = [(i, (i - 1) % count) for i in range(count)]
        return [(up, down), (down, up)]
    first = [(i, i ^ 1) for i in range(count)]
    if count == 2:
        return [(first, first)]
    second = [(i, ((i + 1) if i % 2 else (i - 1)) % count) for i in range(count)]
    pair = [(first, first), (second, second)]
    return pair[::-1] if axis == "plate" else pair


def which_block(shift, axis, count):
    if count == 1:
        return jnp.zeros_like(shift)
    if count == 2:
        return jnp.where(shift == 1, 0, 1)
    odd = 1 if count % 2 else lax.axis_index(axis) % 2
    if axis == "plate" and count % 2 == 0:
        odd = 1 - odd
    return jnp.where(shift == 1, 0, jnp.where(shift == 2, 1 + odd, 2 - odd))


def count_steps(index, step, last):
    out = jnp.zeros_like(index)
    for k in range(1, last):
        out = out + jnp.where(index >= k * step, 1, 0)
    return out


def sigmoid(v):
    return 1.0 / (1.0 + jnp.exp(-v))


def pack_kernel(pos_ref, feat_ref, kind_ref, out_ref, pos_vmem, kind_vmem, sems):
    rows, atoms = feat_ref.shape
    copies = [
        pltpu.make_async_copy(pos_ref, pos_vmem, sems.at[0]),
        pltpu.make_async_copy(kind_ref, kind_vmem, sems.at[1]),
        pltpu.make_async_copy(feat_ref, out_ref.at[pl.ds(EXTRA, rows)], sems.at[2]),
    ]
    for copy in copies:
        copy.start()
    copies[0].wait()
    copies[1].wait()
    pos = jnp.concatenate([pos_vmem[k] for k in range(3)], axis=0)
    high = pos.astype(BF16).astype(F32)
    fill = jnp.zeros((EXTRA - 7, atoms), F32)
    small = jnp.concatenate([high, pos - high, kind_vmem[...].astype(F32), fill], axis=0)
    out_ref[pl.ds(0, EXTRA), :] = small.astype(BF16)
    copies[2].wait()


def pack(positions, features, species):
    rows, atoms = features.shape
    hbm = pl.BlockSpec(memory_space=pltpu.HBM)
    return pl.pallas_call(
        pack_kernel,
        out_shape=jax.ShapeDtypeStruct((rows + EXTRA, atoms), BF16),
        in_specs=[hbm, hbm, hbm],
        out_specs=pl.BlockSpec(memory_space=pltpu.VMEM),
        scratch_shapes=[
            pltpu.VMEM(positions.shape, F32),
            pltpu.VMEM(species.shape, jnp.int32),
            pltpu.SemaphoreType.DMA((3,)),
        ],
        compiler_params=pltpu.CompilerParams(vmem_limit_bytes=4 * 1024 * 1024),
        name="pack",
    )(*(pltpu.with_memory_space_constraint(x, pltpu.HBM) for x in (positions, features, species)))


def prep_kernel(plan, edges_hbm, count_ref, emb_hbm, w1_hbm, w2_hbm, wo_hbm, *refs):
    n_plate, n_column, n_gz, counts, atoms = plan
    held, refs = refs[:n_gz], refs[n_gz:]
    part_i_ref, part_j_ref, hot_i_ref, hot_j_ref, side_ref, emb_ref, w1_ref, w2_ref, wo_ref, edges_ref, row_ref, sems = refs
    pairs = ((edges_hbm, edges_ref), (emb_hbm, emb_ref), (w1_hbm, w1_ref), (w2_hbm, w2_ref), (wo_hbm, row_ref))
    copies = [pltpu.make_async_copy(src, dst, sems.at[k]) for k, (src, dst) in enumerate(pairs)]
    for copy in copies:
        copy.start()
    for copy in copies:
        copy.wait()
    total = edges_ref.shape[1]
    left = edges_ref[0:1, :]
    right = edges_ref[1:2, :]
    side_i = count_steps(left, atoms, 3)
    row_i = which_block(side_i, "plate", counts[0]) * atoms + (left - side_i * atoms)
    blk_j = count_steps(right, atoms, 9)
    u_j = count_steps(blk_j, 3, 3)
    v_j = blk_j - 3 * u_j
    slot_j = which_block(u_j, "tower", counts[1]) * n_gz + which_block(v_j, "gz", counts[2])
    row_j = slot_j * atoms + (right - blk_j * atoms)
    iota_i = lax.broadcasted_iota(jnp.int32, (n_plate * atoms, total), 0)
    hot_i_ref[...] = jnp.where(iota_i == row_i, 1.0, 0.0).astype(BF16)
    iota_j = lax.broadcasted_iota(jnp.int32, (n_column * atoms, total), 0)
    hot_j_ref[...] = jnp.where(iota_j == row_j, 1.0, 0.0).astype(BF16)
    part_i_ref[...] = jnp.dot(held[0][...], hot_i_ref[pl.ds(0, atoms), :], preferred_element_type=F32)
    here = jnp.concatenate([ref[...] for ref in held], axis=1)
    part_j_ref[...] = jnp.dot(here, hot_j_ref[pl.ds(0, n_gz * atoms), :], preferred_element_type=F32)
    slots = lax.broadcasted_iota(jnp.int32, (1, total), 1)
    live = jnp.where(slots < count_ref[0], 1, 0)
    side_ref[...] = jnp.concatenate([side_i - 1, u_j - 1, v_j - 1, live] * 2, axis=0).astype(F32)
    chan = row_ref.shape[1]
    eye = lax.broadcasted_iota(jnp.int32, (chan, chan), 0) == lax.broadcasted_iota(jnp.int32, (chan, chan), 1)
    wo_ref[...] = jnp.sum(jnp.where(eye, row_ref[...].astype(F32), 0.0), axis=1, keepdims=True)


def edge_kernel(plan, *refs):
    n_plate, n_column, n_gz, counts, atoms = plan
    n_far, n_away = n_column - n_gz, n_plate - 1
    far_refs, away_refs, refs = refs[:n_far], refs[n_far : n_far + n_away], refs[n_far + n_away :]
    part_i_ref, part_j_ref, hot_i_ref, hot_j_ref, side_ref, emb_ref, w1_ref, w2_ref, wo_ref = refs[:9]
    energy_ref, plate_ref, column_ref = refs[9:]
    rows, total = part_i_ref.shape
    width = (rows - EXTRA) // 9
    hot_i = hot_i_ref[...]
    hot_j = hot_j_ref[...]

    def gather(part, blocks, hot, start):
        if not blocks:
            return part
        block = jnp.concatenate([ref[...] for ref in blocks], axis=1)
        return part + jnp.dot(block, hot[start * atoms :], preferred_element_type=F32)

    got_i = gather(part_i_ref[...], away_refs, hot_i, 1)
    got_j = gather(part_j_ref[...], far_refs, hot_j, n_gz)

    def row(got, k):
        return got[k : k + 1, :]

    d = []
    for axis in range(3):
        ci = row(got_i, axis) + row(got_i, 3 + axis)
        cj = row(got_j, axis) + row(got_j, 3 + axis)
        off = side_ref[axis : axis + 1, :]
        if axis == 0:
            ci = ci + off
        else:
            cj = cj + off
        d.append(cj - ci)
    r2 = d[0] * d[0] + d[1] * d[1] + d[2] * d[2] + SOFTEN
    r = jnp.sqrt(r2)
    inv = 1.0 / r
    nx, ny, nz = d[0] * inv, d[1] * inv, d[2] * inv
    root3, root5, root15 = math.sqrt(3.0), math.sqrt(5.0), math.sqrt(15.0)
    harm = [
        None,
        root3 * nx,
        root3 * ny,
        root3 * nz,
        root15 * nx * ny,
        root15 * ny * nz,
        0.5 * root5 * (3.0 * nz * nz - 1.0),
        root15 * nx * nz,
        0.5 * root15 * (nx * nx - ny * ny),
    ]
    freq = (lax.broadcasted_iota(jnp.int32, (RB, 1), 0) + 1).astype(F32) * (math.pi / RADIUS)
    phase = freq * r
    radial = jnp.sin(phase) * inv
    wave = jnp.cos(phase)
    gap = jnp.maximum(1.0 - r2 / (RADIUS * RADIUS), 0.0)
    env = gap * gap

    def feat(got, m):
        return got[EXTRA + m * width : EXTRA + (m + 1) * width, :]

    def degrees(got):
        one = harm[1] * feat(got, 1) + harm[2] * feat(got, 2) + harm[3] * feat(got, 3)
        two = harm[4] * feat(got, 4)
        for m in range(5, 9):
            two = two + harm[m] * feat(got, m)
        return feat(got, 0), one, two

    s_i = degrees(got_i)
    s_j = degrees(got_j)
    q = jnp.concatenate([(a * b).astype(BF16) for a, b in zip(s_i, s_j)], axis=0)

    kinds = emb_ref.shape[0]
    kind_iota = lax.broadcasted_iota(jnp.int32, (kinds, total), 0).astype(F32)
    tn = (((0,), (0,)), ((), ()))

    def emb_of(got):
        hot = jnp.where(kind_iota == row(got, 6), 1.0, 0.0).astype(BF16)
        return lax.dot_general(emb_ref[...], hot, tn, preferred_element_type=F32).astype(BF16)

    emb = jnp.concatenate([emb_of(got_i), emb_of(got_j)], axis=0)
    w1 = w1_ref[...]
    w_rad = w1[:RB, :]
    w_emb = w1[RB : RB + 2 * width, :]
    w_q = w1[RB + 2 * width :, :]
    pre1 = (
        lax.dot_general(w_q, q, tn, preferred_element_type=F32)
        + lax.dot_general(w_emb, emb, tn, preferred_element_type=F32)
        + lax.dot_general(w_rad, radial.astype(BF16), tn, preferred_element_type=F32)
    )
    sig1 = sigmoid(pre1)
    hidden = (pre1 * sig1).astype(BF16)
    w2 = w2_ref[...]
    pre2 = jnp.dot(w2, hidden, preferred_element_type=F32)
    sig2 = sigmoid(pre2)
    w_out = wo_ref[...]
    score = jnp.sum(w_out * (pre2 * sig2), axis=0, keepdims=True)
    live = side_ref[3:4, :]
    live_env = live * env
    energy_ref[...] = live_env * score

    g2 = (live_env * w_out) * (sig2 * (1.0 + pre2 * (1.0 - sig2)))
    dh = lax.dot_general(w2, g2.astype(BF16), tn, preferred_element_type=F32).astype(BF16).astype(F32)
    g1 = (dh * (sig1 * (1.0 + pre1 * (1.0 - sig1)))).astype(BF16)
    dq = jnp.dot(w_q, g1, preferred_element_type=F32).astype(BF16).astype(F32)
    dradial = jnp.dot(w_rad, g1, preferred_element_type=F32).astype(BF16).astype(F32)
    dy = [None] * 9
    for deg, members in ((1, range(1, 4)), (2, range(4, 9))):
        part = dq[deg * width : (deg + 1) * width, :]
        for_i = part * s_j[deg]
        for_j = part * s_i[deg]
        for m in members:
            dy[m] = jnp.sum(for_i * feat(got_i, m) + for_j * feat(got_j, m), axis=0, keepdims=True)
    gn = [
        root3 * dy[1] + root15 * (ny * dy[4] + nz * dy[7] + nx * dy[8]),
        root3 * dy[2] + root15 * (nx * dy[4] + nz * dy[5] - ny * dy[8]),
        root3 * dy[3] + root15 * (ny * dy[5] + nx * dy[7]) + (3.0 * root5) * nz * dy[6],
    ]
    dr = jnp.sum(dradial * (freq * wave - radial), axis=0, keepdims=True)
    dr = (dr - (gn[0] * nx + gn[1] * ny + gn[2] * nz)) * inv
    dr2 = dr * (0.5 * inv) - (live * score) * gap * (2.0 / (RADIUS * RADIUS))
    grad = jnp.concatenate([gn[k] * inv + 2.0 * d[k] * dr2 for k in range(3)], axis=0)
    high = grad.astype(BF16).astype(F32)
    both = jnp.concatenate([high, grad - high, jnp.zeros((10, total), F32)], axis=0).astype(BF16)
    nt = (((1,), (1,)), ((), ()))

    def spread(hot):
        out = lax.dot_general(both, hot, nt, preferred_element_type=F32)
        return out[0:3, :] + out[3:6, :]

    to_plate = spread(hot_i)
    to_column = spread(hot_j)
    own = to_plate[:, :atoms] - to_column[:, :atoms]
    for k in range(1, n_plate):
        plate_ref[k - 1] = to_plate[:, k * atoms : (k + 1) * atoms]
    column_ref[0, 0] = own
    for k in range(1, n_column):
        column_ref[k // n_gz, k % n_gz] = -to_column[:, k * atoms : (k + 1) * atoms]


def shards(positions, features, species, emb_table, edges, edge_count, w_first, w_second, w_out):
    atoms = positions.shape[-1]
    total = edges.shape[-1]
    packed = pack(positions.reshape(3, 1, atoms), features[0, 0, 0], species[0, 0])

    plate_moves, tower_moves, gz_moves = moves("plate"), moves("tower"), moves("gz")
    n_gz = 1 + len(gz_moves)
    plate_blocks = [packed] + [lax.ppermute(packed, "plate", there) for there, _ in plate_moves]
    gz_blocks = [packed] + [lax.ppermute(packed, "gz", there) for there, _ in gz_moves]
    near = [[lax.ppermute(b, "tower", there) for b in gz_blocks] for there, _ in tower_moves[:1]]
    relay = list(gz_blocks)
    if near and gz_moves:
        relay[1:] = lax.optimization_barrier((*gz_blocks[1:], near[0][0]))[:-1]
    far = [[lax.ppermute(b, "tower", there) for b in relay] for there, _ in tower_moves[1:]]
    column_blocks = gz_blocks + [b for blocks in near + far for b in blocks]
    n_plate, n_column = len(plate_blocks), len(column_blocks)

    counts = (lax.axis_size("plate"), lax.axis_size("tower"), lax.axis_size("gz"))
    plan = (n_plate, n_column, n_gz, counts, atoms)
    vmem = pl.BlockSpec(memory_space=pltpu.VMEM)
    hbm = pl.BlockSpec(memory_space=pltpu.HBM)
    smem = pl.BlockSpec(memory_space=pltpu.SMEM)
    w_table = w_first.T
    w_row = w_out.reshape(1, -1)
    edge_list = edges[0, 0, 0]
    prepared = pl.pallas_call(
        functools.partial(prep_kernel, plan),
        out_shape=(
            jax.ShapeDtypeStruct((packed.shape[0], total), F32),
            jax.ShapeDtypeStruct((packed.shape[0], total), F32),
            jax.ShapeDtypeStruct((n_plate * atoms, total), BF16),
            jax.ShapeDtypeStruct((n_column * atoms, total), BF16),
            jax.ShapeDtypeStruct((8, total), F32),
            jax.ShapeDtypeStruct(emb_table.shape, BF16),
            jax.ShapeDtypeStruct(w_table.shape, BF16),
            jax.ShapeDtypeStruct(w_second.shape, BF16),
            jax.ShapeDtypeStruct((w_row.shape[1], 1), F32),
        ),
        in_specs=[hbm, smem, hbm, hbm, hbm, hbm] + [vmem] * n_gz,
        out_specs=(vmem,) * 9,
        scratch_shapes=[
            pltpu.VMEM(edge_list.shape, jnp.int32),
            pltpu.VMEM(w_row.shape, BF16),
            pltpu.SemaphoreType.DMA((5,)),
        ],
        compiler_params=pltpu.CompilerParams(vmem_limit_bytes=16 * 1024 * 1024),
        name="prep",
    )(
        pltpu.with_memory_space_constraint(edge_list, pltpu.HBM),
        edge_count.reshape(1),
        *(pltpu.with_memory_space_constraint(w, pltpu.HBM) for w in (emb_table, w_table, w_second, w_row)),
        *gz_blocks,
    )
    energy, plate_part, column_part = pl.pallas_call(
        functools.partial(edge_kernel, plan),
        out_shape=(
            jax.ShapeDtypeStruct((1, total), F32),
            jax.ShapeDtypeStruct((max(n_plate - 1, 1), 3, atoms), F32),
            jax.ShapeDtypeStruct((1 + len(tower_moves), n_gz, 3, atoms), F32),
        ),
        in_specs=[vmem] * (n_plate - 1 + n_column - n_gz + 9),
        out_specs=(vmem, vmem, vmem),
        compiler_params=pltpu.CompilerParams(vmem_limit_bytes=32 * 1024 * 1024),
        name="edge_work",
    )(*column_blocks[n_gz:], *plate_blocks[1:], *prepared)

    forces = 0.0
    for k, (_, back) in enumerate(plate_moves):
        forces = forces + lax.ppermute(plate_part[k], "plate", back)
    column = column_part[:, 0]
    for k, (_, back) in enumerate(gz_moves):
        column = column + lax.ppermute(column_part[:, 1 + k], "gz", back)
    forces = forces + column[0]
    for k, (_, back) in enumerate(tower_moves):
        forces = forces + lax.ppermute(column[1 + k], "tower", back)
    return (forces.reshape(1, 1, 1, 3, atoms), energy.reshape(1, 1, 1, -1))


def solution(mesh):
    placed = (
        P("plate", "tower", "gz", None, None),
        P("plate", "tower", "gz", None, None),
        P("plate", "tower", "gz", None),
        P(),
        P("plate", "tower", "gz", None, None),
        P("plate", "tower", "gz"),
        P(),
        P(),
        P(),
    )
    return jax.shard_map(
        shards,
        mesh=mesh,
        in_specs=placed,
        out_specs=(P("plate", "tower", "gz", None, None), P("plate", "tower", "gz", None)),
        check_vma=False,
    )
```

```python
import functools
import math

import jax
import jax.numpy as jnp
from jax import lax
from jax.experimental import pallas as pl
from jax.experimental.pallas import tpu as pltpu
from jax.sharding import PartitionSpec as P

RB = 8
RADIUS = 3.0
SOFTEN = 0.04
EXTRA = 16
F32 = jnp.float32
BF16 = jnp.bfloat16


def moves(axis):
    count = lax.axis_size(axis)
    if count == 1:
        return []
    if count % 2:
        up = [(i, (i + 1) % count) for i in range(count)]
        down = [(i, (i - 1) % count) for i in range(count)]
        return [(up, down), (down, up)]
    first = [(i, i ^ 1) for i in range(count)]
    if count == 2:
        return [(first, first)]
    second = [(i, ((i + 1) if i % 2 else (i - 1)) % count) for i in range(count)]
    pair = [(first, first), (second, second)]
    return pair[::-1] if axis in ("plate", "tower") else pair


def which_block(shift, axis, count):
    if count == 1:
        return jnp.zeros_like(shift)
    if count == 2:
        return jnp.where(shift == 1, 0, 1)
    odd = 1 if count % 2 else lax.axis_index(axis) % 2
    if axis in ("plate", "tower") and count % 2 == 0:
        odd = 1 - odd
    return jnp.where(shift == 1, 0, jnp.where(shift == 2, 1 + odd, 2 - odd))


def count_steps(index, step, last):
    out = jnp.zeros_like(index)
    for k in range(1, last):
        out = out + jnp.where(index >= k * step, 1, 0)
    return out


def sigmoid(v):
    return 0.5 + 0.5 * jnp.tanh(0.5 * v)


def pack_kernel(pos_ref, feat_ref, kind_ref, out_ref, pos_vmem, kind_vmem, sems):
    rows, atoms = feat_ref.shape
    copies = [
        pltpu.make_async_copy(pos_ref, pos_vmem, sems.at[0]),
        pltpu.make_async_copy(kind_ref, kind_vmem, sems.at[1]),
        pltpu.make_async_copy(feat_ref, out_ref.at[pl.ds(EXTRA, rows)], sems.at[2]),
    ]
    for copy in copies:
        copy.start()
    copies[0].wait()
    copies[1].wait()
    pos = jnp.concatenate([pos_vmem[k] for k in range(3)], axis=0)
    high = pos.astype(BF16).astype(F32)
    fill = jnp.zeros((EXTRA - 7, atoms), F32)
    small = jnp.concatenate([high, pos - high, kind_vmem[...].astype(F32), fill], axis=0)
    out_ref[pl.ds(0, EXTRA), :] = small.astype(BF16)
    copies[2].wait()


def pack(positions, features, species):
    rows, atoms = features.shape
    hbm = pl.BlockSpec(memory_space=pltpu.HBM)
    return pl.pallas_call(
        pack_kernel,
        out_shape=jax.ShapeDtypeStruct((rows + EXTRA, atoms), BF16),
        in_specs=[hbm, hbm, hbm],
        out_specs=pl.BlockSpec(memory_space=pltpu.VMEM),
        scratch_shapes=[
            pltpu.VMEM(positions.shape, F32),
            pltpu.VMEM(species.shape, jnp.int32),
            pltpu.SemaphoreType.DMA((3,)),
        ],
        compiler_params=pltpu.CompilerParams(vmem_limit_bytes=4 * 1024 * 1024),
        name="pack",
    )(*(pltpu.with_memory_space_constraint(x, pltpu.HBM) for x in (positions, features, species)))


def prep_kernel(plan, edges_hbm, count_ref, emb_hbm, w1_hbm, w2_hbm, wo_hbm, *refs):
    n_plate, n_column, n_gz, counts, atoms = plan
    held, refs = refs[:n_gz], refs[n_gz:]
    part_i_ref, part_j_ref, hot_i_ref, hot_j_ref, side_ref, emb_ref, w1_ref, w2_ref, wo_ref, edges_ref, row_ref, sems = refs
    pairs = ((edges_hbm, edges_ref), (emb_hbm, emb_ref), (w1_hbm, w1_ref), (w2_hbm, w2_ref), (wo_hbm, row_ref))
    copies = [pltpu.make_async_copy(src, dst, sems.at[k]) for k, (src, dst) in enumerate(pairs)]
    for copy in copies:
        copy.start()
    for copy in copies:
        copy.wait()
    total = edges_ref.shape[1]
    left = edges_ref[0:1, :]
    right = edges_ref[1:2, :]
    side_i = count_steps(left, atoms, 3)
    row_i = which_block(side_i, "plate", counts[0]) * atoms + (left - side_i * atoms)
    blk_j = count_steps(right, atoms, 9)
    u_j = count_steps(blk_j, 3, 3)
    v_j = blk_j - 3 * u_j
    slot_j = which_block(u_j, "tower", counts[1]) * n_gz + which_block(v_j, "gz", counts[2])
    row_j = slot_j * atoms + (right - blk_j * atoms)
    iota_i = lax.broadcasted_iota(jnp.int32, (n_plate * atoms, total), 0)
    hot_i_ref[...] = jnp.where(iota_i == row_i, 1.0, 0.0).astype(BF16)
    iota_j = lax.broadcasted_iota(jnp.int32, (n_column * atoms, total), 0)
    hot_j_ref[...] = jnp.where(iota_j == row_j, 1.0, 0.0).astype(BF16)
    part_i_ref[...] = jnp.dot(held[0][...], hot_i_ref[pl.ds(0, atoms), :], preferred_element_type=F32)
    here = jnp.concatenate([ref[...] for ref in held], axis=1)
    part_j_ref[...] = jnp.dot(here, hot_j_ref[pl.ds(0, n_gz * atoms), :], preferred_element_type=F32)
    slots = lax.broadcasted_iota(jnp.int32, (1, total), 1)
    live = jnp.where(slots < count_ref[0], 1, 0)
    side_ref[...] = jnp.concatenate([side_i - 1, u_j - 1, v_j - 1, live] * 2, axis=0).astype(F32)
    chan = row_ref.shape[1]
    eye = lax.broadcasted_iota(jnp.int32, (chan, chan), 0) == lax.broadcasted_iota(jnp.int32, (chan, chan), 1)
    wo_ref[...] = jnp.sum(jnp.where(eye, row_ref[...].astype(F32), 0.0), axis=1, keepdims=True)


def edge_part(lanes, size, rows, width, atoms, n_gz, away, far, inputs, energy_ref, out):
    part_i_ref, part_j_ref, hot_i_ref, hot_j_ref, side_ref, emb_ref, w1_ref, w2_ref, wo_ref = inputs

    def gather(part, block, hot, start):
        if block is None:
            return part
        return part + jnp.dot(block, hot[start * atoms :, lanes], preferred_element_type=F32)

    got_i = gather(part_i_ref[:, lanes], away, hot_i_ref, 1)
    got_j = gather(part_j_ref[:, lanes], far, hot_j_ref, n_gz)
    yield

    def row(got, k):
        return got[k : k + 1, :]

    d = []
    for axis in range(3):
        ci = row(got_i, axis) + row(got_i, 3 + axis)
        cj = row(got_j, axis) + row(got_j, 3 + axis)
        off = side_ref[axis : axis + 1, lanes]
        if axis == 0:
            ci = ci + off
        else:
            cj = cj + off
        d.append(cj - ci)
    r2 = d[0] * d[0] + d[1] * d[1] + d[2] * d[2] + SOFTEN
    inv = lax.rsqrt(r2)
    r = r2 * inv
    nx, ny, nz = d[0] * inv, d[1] * inv, d[2] * inv
    root3, root5, root15 = math.sqrt(3.0), math.sqrt(5.0), math.sqrt(15.0)
    harm = [
        None,
        root3 * nx,
        root3 * ny,
        root3 * nz,
        root15 * nx * ny,
        root15 * ny * nz,
        0.5 * root5 * (3.0 * nz * nz - 1.0),
        root15 * nx * nz,
        0.5 * root15 * (nx * nx - ny * ny),
    ]
    freq = (lax.broadcasted_iota(jnp.int32, (RB, 1), 0) + 1).astype(F32) * (math.pi / RADIUS)
    phase = freq * r
    radial = jnp.sin(phase) * inv
    wave = jnp.cos(phase)
    gap = jnp.maximum(1.0 - r2 / (RADIUS * RADIUS), 0.0)
    env = gap * gap

    def feat(got, m):
        return got[EXTRA + m * width : EXTRA + (m + 1) * width, :]

    def degrees(got):
        one = harm[1] * feat(got, 1) + harm[2] * feat(got, 2) + harm[3] * feat(got, 3)
        two = harm[4] * feat(got, 4)
        for m in range(5, 9):
            two = two + harm[m] * feat(got, m)
        return feat(got, 0), one, two

    s_i = degrees(got_i)
    s_j = degrees(got_j)
    q = jnp.concatenate([(a * b).astype(BF16) for a, b in zip(s_i, s_j)], axis=0)

    yield
    kinds = emb_ref.shape[0]
    kind_iota = lax.broadcasted_iota(jnp.int32, (kinds, size), 0).astype(F32)
    tn = (((0,), (0,)), ((), ()))

    def emb_of(got):
        hot = jnp.where(kind_iota == row(got, 6), 1.0, 0.0).astype(BF16)
        return lax.dot_general(emb_ref[...], hot, tn, preferred_element_type=F32).astype(BF16)

    emb = jnp.concatenate([emb_of(got_i), emb_of(got_j)], axis=0)
    w1 = w1_ref[...]
    w_rad = w1[:RB, :]
    w_emb = w1[RB : RB + 2 * width, :]
    w_q = w1[RB + 2 * width :, :]
    pre1 = (
        lax.dot_general(w_q, q, tn, preferred_element_type=F32)
        + lax.dot_general(w_emb, emb, tn, preferred_element_type=F32)
        + lax.dot_general(w_rad, radial.astype(BF16), tn, preferred_element_type=F32)
    )
    yield
    sig1 = sigmoid(pre1)
    hidden = (pre1 * sig1).astype(BF16)
    w2 = w2_ref[...]
    pre2 = jnp.dot(w2, hidden, preferred_element_type=F32)
    yield
    sig2 = sigmoid(pre2)
    w_out = wo_ref[...]
    score = jnp.sum(w_out * (pre2 * sig2), axis=0, keepdims=True)
    live = side_ref[3:4, lanes]
    live_env = live * env
    energy_ref[:, lanes] = live_env * score

    g2 = (live_env * w_out) * (sig2 * (1.0 + pre2 * (1.0 - sig2)))
    dh = lax.dot_general(w2, g2.astype(BF16), tn, preferred_element_type=F32).astype(BF16).astype(F32)
    yield
    g1 = (dh * (sig1 * (1.0 + pre1 * (1.0 - sig1)))).astype(BF16)
    dq = jnp.dot(w_q, g1, preferred_element_type=F32).astype(BF16).astype(F32)
    dradial = jnp.dot(w_rad, g1, preferred_element_type=F32).astype(BF16).astype(F32)
    yield
    dy = [None] * 9
    for deg, members in ((1, range(1, 4)), (2, range(4, 9))):
        part = dq[deg * width : (deg + 1) * width, :]
        for_i = part * s_j[deg]
        for_j = part * s_i[deg]
        for m in members:
            both = for_i * feat(got_i, m) + for_j * feat(got_j, m)
            dy[m] = jnp.sum(both.reshape(width // 8, 8, size), axis=0)
    gn = [jnp.sum(term, axis=0, keepdims=True) for term in (
        root3 * dy[1] + root15 * (ny * dy[4] + nz * dy[7] + nx * dy[8]),
        root3 * dy[2] + root15 * (nx * dy[4] + nz * dy[5] - ny * dy[8]),
        root3 * dy[3] + root15 * (ny * dy[5] + nx * dy[7]) + (3.0 * root5) * nz * dy[6],
    )]
    dr = jnp.sum(dradial * (freq * wave - radial), axis=0, keepdims=True)
    dr = (dr - (gn[0] * nx + gn[1] * ny + gn[2] * nz)) * inv
    dr2 = dr * (0.5 * inv) - (live * score) * gap * (2.0 / (RADIUS * RADIUS))
    grad = jnp.concatenate([gn[k] * inv + 2.0 * d[k] * dr2 for k in range(3)], axis=0)
    high = grad.astype(BF16).astype(F32)
    both = jnp.concatenate([high, grad - high, jnp.zeros((10, size), F32)], axis=0).astype(BF16)
    out.append(both)


def unsort(order, refs):
    out = [None] * len(order)
    for place, k in enumerate(order):
        out[k] = refs[place]
    return out


def edge_kernel(plan, order, *refs):
    n_plate, n_column, n_gz, counts, atoms = plan
    n_far, n_away = n_column - n_gz, n_plate - 1
    arrived = unsort(order, refs)
    far_refs, away_refs, refs = arrived[:n_far], arrived[n_far:], refs[n_far + n_away :]
    inputs = refs[:9]
    part_i_ref, _, hot_i_ref, hot_j_ref = inputs[:4]
    energy_ref, plate_ref, column_ref = refs[9:]
    rows, total = part_i_ref.shape
    width = (rows - EXTRA) // 9
    def lay(refs):
        return jnp.concatenate([ref[...] for ref in refs], axis=1) if refs else None

    away, far = lay(away_refs), lay(far_refs)
    pieces = 2 if total % (128 * 2) == 0 else 1
    size = total // pieces
    outs = [[] for _ in range(pieces)]
    steps = [
        edge_part(slice(k * size, (k + 1) * size), size, rows, width, atoms, n_gz, away, far, inputs, energy_ref, outs[k])
        for k in range(pieces)
    ]
    running = [True] * pieces
    while any(running):
        for k, step in enumerate(steps):
            if running[k]:
                running[k] = next(step, "end") != "end"
    both = jnp.concatenate([out[0] for out in outs], axis=1)
    hot_i, hot_j = hot_i_ref[...], hot_j_ref[...]
    nt = (((1,), (1,)), ((), ()))

    def spread(hot):
        out = lax.dot_general(both, hot, nt, preferred_element_type=F32)
        return out[0:3, :] + out[3:6, :]

    to_plate = spread(hot_i)
    to_column = spread(hot_j)
    own = to_plate[:, :atoms] - to_column[:, :atoms]
    for k in range(1, n_plate):
        plate_ref[k - 1] = to_plate[:, k * atoms : (k + 1) * atoms]
    column_ref[0, 0] = own
    for k in range(1, n_column):
        column_ref[k // n_gz, k % n_gz] = -to_column[:, k * atoms : (k + 1) * atoms]


def shards(positions, features, species, emb_table, edges, edge_count, w_first, w_second, w_out):
    atoms = positions.shape[-1]
    total = edges.shape[-1]
    packed = pack(positions.reshape(3, 1, atoms), features[0, 0, 0], species[0, 0])

    plate_moves, tower_moves, gz_moves = moves("plate"), moves("tower"), moves("gz")
    n_gz = 1 + len(gz_moves)
    plate_blocks = [packed] + [lax.ppermute(packed, "plate", there) for there, _ in plate_moves]
    gz_blocks = [packed] + [lax.ppermute(packed, "gz", there) for there, _ in gz_moves]
    near = [[lax.ppermute(b, "tower", there) for b in gz_blocks] for there, _ in tower_moves[:1]]
    far = [[lax.ppermute(b, "tower", there) for b in gz_blocks] for there, _ in tower_moves[1:]]
    column_blocks = gz_blocks + [b for blocks in near + far for b in blocks]
    n_plate, n_column = len(plate_blocks), len(column_blocks)

    counts = (lax.axis_size("plate"), lax.axis_size("tower"), lax.axis_size("gz"))
    plan = (n_plate, n_column, n_gz, counts, atoms)
    vmem = pl.BlockSpec(memory_space=pltpu.VMEM)
    hbm = pl.BlockSpec(memory_space=pltpu.HBM)
    smem = pl.BlockSpec(memory_space=pltpu.SMEM)
    w_table = w_first.T
    w_row = w_out.reshape(1, -1)
    edge_list = edges[0, 0, 0]
    prepared = pl.pallas_call(
        functools.partial(prep_kernel, plan),
        out_shape=(
            jax.ShapeDtypeStruct((packed.shape[0], total), F32),
            jax.ShapeDtypeStruct((packed.shape[0], total), F32),
            jax.ShapeDtypeStruct((n_plate * atoms, total), BF16),
            jax.ShapeDtypeStruct((n_column * atoms, total), BF16),
            jax.ShapeDtypeStruct((8, total), F32),
            jax.ShapeDtypeStruct(emb_table.shape, BF16),
            jax.ShapeDtypeStruct(w_table.shape, BF16),
            jax.ShapeDtypeStruct(w_second.shape, BF16),
            jax.ShapeDtypeStruct((w_row.shape[1], 1), F32),
        ),
        in_specs=[hbm, smem, hbm, hbm, hbm, hbm] + [vmem] * n_gz,
        out_specs=(vmem,) * 9,
        scratch_shapes=[
            pltpu.VMEM(edge_list.shape, jnp.int32),
            pltpu.VMEM(w_row.shape, BF16),
            pltpu.SemaphoreType.DMA((5,)),
        ],
        compiler_params=pltpu.CompilerParams(vmem_limit_bytes=16 * 1024 * 1024),
        name="prep",
    )(
        pltpu.with_memory_space_constraint(edge_list, pltpu.HBM),
        edge_count.reshape(1),
        *(pltpu.with_memory_space_constraint(w, pltpu.HBM) for w in (emb_table, w_table, w_second, w_row)),
        *gz_blocks,
    )
    arrived = column_blocks[n_gz:] + plate_blocks[1:]
    groups = [("ac", "bd")[m > 0][k] for k in range(len(tower_moves)) for m in range(n_gz)] + list("ef"[: n_plate - 1])
    order = sorted(range(len(arrived)), key=lambda k: "cdfaeb".index(groups[k]))
    energy, plate_part, column_part = pl.pallas_call(
        functools.partial(edge_kernel, plan, order),
        out_shape=(
            jax.ShapeDtypeStruct((1, total), F32),
            jax.ShapeDtypeStruct((max(n_plate - 1, 1), 3, atoms), F32),
            jax.ShapeDtypeStruct((1 + len(tower_moves), n_gz, 3, atoms), F32),
        ),
        in_specs=[vmem] * (n_plate - 1 + n_column - n_gz + 9),
        out_specs=(vmem, vmem, vmem),
        compiler_params=pltpu.CompilerParams(vmem_limit_bytes=32 * 1024 * 1024),
        name="edge_work",
    )(*(arrived[k] for k in order), *prepared)

    forces = 0.0
    for k, (_, back) in enumerate(plate_moves):
        forces = forces + lax.ppermute(plate_part[k], "plate", back)
    column = column_part[:, 0]
    for k, (_, back) in enumerate(gz_moves):
        column = column + lax.ppermute(column_part[:, 1 + k], "gz", back)
    forces = forces + column[0]
    for k, (_, back) in enumerate(tower_moves):
        forces = forces + lax.ppermute(column[1 + k], "tower", back)
    return (forces.reshape(1, 1, 1, 3, atoms), energy.reshape(1, 1, 1, -1))


def solution(mesh):
    placed = (
        P("plate", "tower", "gz", None, None),
        P("plate", "tower", "gz", None, None),
        P("plate", "tower", "gz", None),
        P(),
        P("plate", "tower", "gz", None, None),
        P("plate", "tower", "gz"),
        P(),
        P(),
        P(),
    )
    return jax.shard_map(
        shards,
        mesh=mesh,
        in_specs=placed,
        out_specs=(P("plate", "tower", "gz", None, None), P("plate", "tower", "gz", None)),
        check_vma=False,
    )
```
